32 devices in a mesh: tm: 4 (over z), ha: 2 (over y), wa: 4 (over x, core).
Axes of the slice: x: 2, y: 2, z: 4, core: 2. Of those that a mesh axis runs over, the one named last changes fastest.
Arguments:
- latent: bfloat16 [8, 32, 64, 512], P('tm', 'ha', 'wa'), may hold values from -1300 to 1300
- norm_gain: float32 [512], replicated, may hold values from 0.1 to 1.9
- norm_bias: float32 [512], replicated, may hold values from -3 to 3
- conv_weight: bfloat16 [3, 3, 3, 512, 256], replicated, may hold values from -0.0546875 to 0.0546875
- conv_bias: float32 [256], replicated, may hold values from -3 to 3
- up_weight: bfloat16 [4, 4, 256, 256], replicated, may hold values from -0.1875 to 0.1875
- up_bias: float32 [256], replicated, may hold values from -3 to 3
Outputs:
- video: bfloat16 [8, 64, 128, 256], P('tm', 'ha', 'wa')
The draws below stay inside these ranges and needn't reach their ends.
All inputs are finite; a program needn't handle non-finite values.
Results may differ from the reference program's by a relative error of at most 0.0054.
Values may be sent and summed in bfloat16 or wider, within the bound.
A program may use at most 64 MiB of HBM per device.

```python
import math
import jax
import jax.numpy as jnp
from jax import lax

C_IN = 512
C_OUT = 256
GROUPS = 32
TF = 2
NF = 8
NH = 32
NW = 64
GROUP_CH = 16
N_TM = 4


def draw_latent(key, part):
    keys = jax.random.split(key, 6)
    shape = (NF, NH, NW, C_IN)
    chan_scale = jnp.exp(jax.random.uniform(keys[1], (C_IN,), minval=0.0, maxval=math.log(10.0)))
    frame_pos = jnp.arange(NF).astype(jnp.float32) / float(max(NF - 1, 1))
    frame_scale = jnp.exp(frame_pos * math.log(3.0) + jax.random.uniform(keys[2], (NF,), minval=-0.35, maxval=0.35))
    row_frac = (jnp.arange(NH).astype(jnp.float32) + 0.5) / float(NH)
    col_frac = (jnp.arange(NW).astype(jnp.float32) + 0.5) / float(NW)
    phases = jax.random.uniform(keys[4], (3,), minval=0.0, maxval=2.0 * math.pi)
    row_log = 0.5 * (2.0 * row_frac - 1.0) + 0.25 * jnp.sin(3.0 * math.pi * row_frac + phases[0])
    col_log = 0.5 * (2.0 * col_frac - 1.0) + 0.25 * jnp.sin(3.0 * math.pi * col_frac + phases[1])
    spatial = jnp.exp(row_log[:, None] + col_log[None, :])
    chan_sign = jax.random.uniform(keys[5], (C_IN,), minval=-1.0, maxval=1.0)
    drift = 0.6 * jnp.sin(2.0 * math.pi * (row_frac[:, None] + 0.5 * col_frac[None, :]) + phases[2])
    shifted = drift[:, :, None] * chan_sign
    base = jnp.clip(jax.random.normal(keys[0], shape), -6.0, 6.0)
    base = base + shifted
    return (base * frame_scale[:, None, None, None] * spatial[:, :, None] * chan_scale).astype(jnp.bfloat16)


def gaussian(stream_key, extent, scale, reach, held_as=jnp.bfloat16):
    return jnp.clip(scale * jax.random.normal(stream_key, extent, jnp.float32), -reach, reach).astype(held_as)


def setup_inputs(seed: int = 0) -> dict:
    seeds = jax.random.split(jax.random.key(seed), 8)
    return {
        "latent": draw_latent(jax.random.fold_in(seeds[7], 71), 0),
        "norm_gain": jnp.clip(1.0 + 0.18 * jax.random.normal(seeds[1], (C_IN,), jnp.float32), 0.1, 1.9),
        "norm_bias": gaussian(seeds[2], (C_IN,), 0.5, 3.0, jnp.float32),
        "conv_weight": gaussian(seeds[3], (3, 3, 3, C_IN, C_OUT), (27 * C_IN) ** -0.5, 0.0546875),
        "conv_bias": gaussian(seeds[4], (C_OUT,), 0.5, 3.0, jnp.float32),
        "up_weight": gaussian(seeds[5], (4, 4, C_OUT, C_OUT), (4 * C_OUT) ** -0.5, 0.1875),
        "up_bias": gaussian(seeds[6], (C_OUT,), 0.5, 3.0, jnp.float32),
    }


def spread_frame(frame, up_weight):
    height, breadth, chans = frame.shape
    flat = frame.reshape(height * breadth, chans).astype(jnp.float32)
    kernels = up_weight.astype(jnp.float32)
    rows_out = []
    for row_par in (0, 1):
        cols_out = []
        for col_par in (0, 1):
            joined = jnp.concatenate([kernels[row_par + 2 * shift_row, col_par + 2 * shift_col] for shift_row in (0, 1) for shift_col in (0, 1)], axis=1)
            product = jnp.dot(flat, joined, precision=lax.Precision.HIGHEST).reshape(height, breadth, 4, chans)
            summed = jnp.zeros((height + 1, breadth + 1, chans), jnp.float32)
            for shift_row in (0, 1):
                for shift_col in (0, 1):
                    summed = summed + jnp.pad(product[:, :, 2 * shift_row + shift_col], ((shift_row, 1 - shift_row), (shift_col, 1 - shift_col), (0, 0)))
            cols_out.append(summed)
        rows_out.append(jnp.stack(cols_out, axis=2))
    return jnp.stack(rows_out, axis=1).reshape(2 * height + 2, 2 * breadth + 2, chans)

def reference(latent, norm_gain, norm_bias, conv_weight, conv_bias, up_weight, up_bias):

    def frame_totals(frame):
        wide = frame.astype(jnp.float32)
        return (lax.optimization_barrier(jnp.sum(wide, axis=(0, 1))), lax.optimization_barrier(jnp.sum(wide * wide, axis=(0, 1))))
    sums, squares = lax.map(frame_totals, latent)
    sums = jnp.cumsum(sums.reshape(N_TM, TF, GROUPS, GROUP_CH).sum(axis=(1, 3)), axis=0)
    squares = jnp.cumsum(squares.reshape(N_TM, TF, GROUPS, GROUP_CH).sum(axis=(1, 3)), axis=0)
    counted = (jnp.arange(N_TM).astype(jnp.float32) + 1.0) * float(TF * NH * NW * GROUP_CH)
    mean = sums / counted[:, None]
    variance = squares / counted[:, None] - mean * mean
    inverse = lax.rsqrt(variance + 1e-06)
    mean_frames = jnp.repeat(jnp.repeat(mean, GROUP_CH, axis=1), TF, axis=0)
    inverse_frames = jnp.repeat(jnp.repeat(inverse, GROUP_CH, axis=1), TF, axis=0)

    def normalize(operands):
        frame, centre, inverse_row = operands
        return jax.nn.silu((frame.astype(jnp.float32) - centre) * inverse_row * norm_gain + norm_bias).astype(jnp.bfloat16)
    normed = lax.map(normalize, (latent, mean_frames, inverse_frames))
    padded = jnp.concatenate([normed[:1], normed[:1], normed], axis=0)
    kernel = conv_weight.astype(jnp.float32)

    def convolve(frame_id):
        window = lax.dynamic_slice_in_dim(padded, frame_id, 3, 0).astype(jnp.float32)[None]
        result = lax.conv_general_dilated(window, kernel, (1, 1, 1), ((0, 0), (1, 1), (1, 1)), dimension_numbers=('NDHWC', 'DHWIO', 'NDHWC'), precision=lax.Precision.HIGHEST)
        return (result[0, 0] + conv_bias).astype(jnp.bfloat16)
    features = lax.map(convolve, jnp.arange(NF).astype(jnp.int32))

    def upsample(frame):
        spread = spread_frame(frame, up_weight)
        return (spread[1:2 * NH + 1, 1:2 * NW + 1] + up_bias).astype(jnp.bfloat16)
    return lax.map(upsample, features)
```

```python
import functools

import jax
import jax.numpy as jnp
from jax import lax
from jax.experimental import pallas as pl
from jax.experimental.pallas import tpu as pltpu
from jax.sharding import PartitionSpec as P

GROUPS = 32
MESH = pl.DeviceIdType.MESH
DIRS = ((-1, 0), (1, 0), (0, -1), (0, 1), (-1, -1), (-1, 1), (1, -1), (1, 1))
KW_ORDER = (3, 1, 2, 0)


def section_kernel(
    n_tm, n_ha, n_wa,
    lat, gain, nbias, wconv_hbm, cbias, wup_hbm, ubias,
    out,
    wconv, wup, sums, plane_stats, block_stats,
    col_out, corner_out, row_in, col_in, corner_in, halo_norm, norm,
    acc0, acc1, part_out, part_in,
    feat, fcol_out, fcorner_out, frow_in, fcol_in, fcorner_in, fpad, spread,
    wsem, usem, pl_send, pl_recv, tm_send, tm_recv, h_send, h_recv, p_send, p_recv, f_send, f_recv,
):
    f32, bf16 = jnp.float32, jnp.bfloat16
    frames, height, breadth, chans = lat.shape
    couts = cbias.shape[-1]
    k, h, w = lax.axis_index("tm"), lax.axis_index("ha"), lax.axis_index("wa")
    n_plane = n_ha * n_wa
    me = h * n_wa + w

    conv_copies = [
        pltpu.make_async_copy(wconv_hbm.at[lag], wconv.at[lag], wsem.at[lag]) for lag in range(3)
    ]
    up_copies = [
        pltpu.make_async_copy(wup_hbm.at[:, kw], wup.at[:, slot], usem.at[slot])
        for slot, kw in enumerate(KW_ORDER)
    ]

    def plane_peer(d):
        q = lax.rem(me + d, n_plane)
        return q, (k, q // n_wa, lax.rem(q, n_wa))

    barrier = pltpu.get_barrier_semaphore()
    for d in range(1, n_plane):
        pl.semaphore_signal(barrier, inc=1, device_id=plane_peer(d)[1], device_id_type=MESH)
    for d in range(1, n_tm):
        pl.semaphore_signal(
            barrier, inc=1, device_id=(lax.rem(k + d, n_tm), h, w), device_id_type=MESH
        )
    for copy in conv_copies + up_copies:
        copy.start()

    def add_row(i, carry):
        total, square = carry
        t, r = i // height, lax.rem(i, height)
        row = lat[t, r].astype(f32)
        col_out[0, t, pl.ds(r, 1), :] = row[0:1]
        col_out[1, t, pl.ds(r, 1), :] = row[breadth - 1 : breadth]
        return total + row, square + row * row

    zero = jnp.zeros((breadth, chans), f32)
    total, square = lax.fori_loop(0, frames * height, add_row, (zero, zero), unroll=4)
    sums[0:1, :] = jnp.sum(total, axis=0, keepdims=True)
    sums[1:2, :] = jnp.sum(square, axis=0, keepdims=True)
    for i, (dy, dx) in enumerate(DIRS[4:]):
        r = 0 if dy < 0 else height - 1
        corner_out[i] = col_out[0 if dx < 0 else 1, :, r, :]
    pl.semaphore_wait(barrier, n_plane - 1 + n_tm - 1)

    def plane_copy(d, slot):
        q, where = plane_peer(d)
        index = me if slot is None else slot
        return pltpu.make_async_remote_copy(
            src_ref=sums, dst_ref=plane_stats.at[index], send_sem=pl_send.at[d],
            recv_sem=pl_recv.at[index], device_id=where, device_id_type=MESH,
        )

    for d in range(1, n_plane):
        plane_copy(d, None).start()
    plane_stats[me] = sums[...]

    def exists(dy, dx):
        ok = None
        for here, step, count in ((h, dy, n_ha), (w, dx, n_wa)):
            if step:
                one = (here + step >= 0) & (here + step < count)
                ok = one if ok is None else ok & one
        return ok

    def halo_copies(tile, cols, corners, rin, cin, kin, send, recv):
        made = []
        for i, (dy, dx) in enumerate(DIRS):
            if dx == 0:
                src, dst = tile.at[:, 0 if dy < 0 else height - 1], rin.at[1 if dy < 0 else 0]
            elif dy == 0:
                src, dst = cols.at[0 if dx < 0 else 1], cin.at[1 if dx < 0 else 0]
            else:
                src, dst = corners.at[i - 4], kin.at[7 - i]
            made.append((dy, dx, pltpu.make_async_remote_copy(
                src_ref=src, dst_ref=dst, send_sem=send.at[i], recv_sem=recv.at[i],
                device_id=(k, h + dy, w + dx), device_id_type=MESH,
            )))
        return made

    def start_all(made):
        for dy, dx, copy in made:
            pl.when(exists(dy, dx))(copy.start)

    def wait_send_all(made):
        for dy, dx, copy in made:
            pl.when(exists(dy, dx))(copy.wait_send)

    def wait_recv_all(made):
        for dy, dx, copy in made:
            pl.when(exists(-dy, -dx))(copy.wait_recv)

    halos = halo_copies(lat, col_out, corner_out, row_in, col_in, corner_in, h_send, h_recv)
    start_all(halos)

    for d in range(1, n_plane):
        plane_copy(d, plane_peer(d)[0]).wait_recv()
    block = plane_stats[0]
    for q in range(1, n_plane):
        block = block + plane_stats[q]
    block_stats[k] = block

    def tm_copy(d, slot):
        return pltpu.make_async_remote_copy(
            src_ref=block_stats.at[k], dst_ref=block_stats.at[slot], send_sem=tm_send.at[d],
            recv_sem=tm_recv.at[slot], device_id=(lax.rem(k + d, n_tm), h, w), device_id_type=MESH,
        )

    for d in range(1, n_tm):
        pl.when(k + d < n_tm)(tm_copy(d, k).start)
    wait_recv_all(halos)
    for d in range(1, n_tm):
        pl.when(k >= d)(tm_copy(d, lax.rem(k + n_tm - d, n_tm)).wait_recv)
    upto = block
    for q in range(n_tm):
        upto = upto + jnp.where(q < k, block_stats[q], 0.0)
    lane = lax.broadcasted_iota(jnp.int32, upto.shape, 1)
    group_width = chans // GROUPS
    step = 1
    while step < group_width:
        ahead = pltpu.roll(upto, chans - step, 1)
        behind = pltpu.roll(upto, step, 1)
        upto = upto + jnp.where((lane & step) == 0, ahead, behind)
        step *= 2
    cells = float(frames * height * breadth * n_plane * group_width)
    stats = upto / ((k + 1).astype(f32) * cells)
    mean = stats[0:1]
    variance = stats[1:2] - mean * mean
    half_scale = 0.5 * (lax.rsqrt(variance + 1e-06) * gain[...])
    half_bias = 0.5 * nbias[...]

    def normed(x):
        half = (x - mean) * half_scale + half_bias
        return half + half * jnp.tanh(half)

    up_ok, down_ok, left_ok, right_ok = exists(-1, 0), exists(1, 0), exists(0, -1), exists(0, 1)
    for side, ok in ((0, left_ok), (1, right_ok)):
        for t in range(frames):
            halo_norm[side, t, 1 : height + 1, :] = jnp.where(ok, normed(col_in[side, t]), 0.0)
    for i, (dy, dx) in enumerate(DIRS[4:]):
        row = 0 if dy < 0 else height + 1
        value = jnp.where(exists(dy, dx), normed(corner_in[i]), 0.0)
        for t in range(frames):
            halo_norm[0 if dx < 0 else 1, t, row : row + 1, :] = value[t : t + 1]

    def put_row(dest, t, r, y, left, right):
        column = lax.broadcasted_iota(jnp.int32, y.shape, 0)
        size = y.shape[1]
        dest[t, r, :, 0:size] = jnp.where(column == 0, left, pltpu.roll(y, 1, 0)).astype(bf16)
        dest[t, r, :, size : 2 * size] = y.astype(bf16)
        dest[t, r, :, 2 * size :] = jnp.where(
            column == breadth - 1, right, pltpu.roll(y, breadth - 1, 0)
        ).astype(bf16)

    def norm_row(i, carry):
        t, r = i // height, lax.rem(i, height)
        put_row(
            norm, t, r + 1, normed(lat[t, r].astype(f32)),
            halo_norm[0, t, pl.ds(r + 1, 1), :], halo_norm[1, t, pl.ds(r + 1, 1), :],
        )
        return carry

    lax.fori_loop(0, frames * height, norm_row, 0, unroll=2)
    for side, row, ok in ((0, 0, up_ok), (1, height + 1, down_ok)):
        for t in range(frames):
            put_row(
                norm, t, row, jnp.where(ok, normed(row_in[side, t].astype(f32)), 0.0),
                halo_norm[0, t, row : row + 1, :], halo_norm[1, t, row : row + 1, :],
            )

    cells_out = height * breadth

    def conv(first, last, lag):
        acc = None
        for dy in range(3):
            left = norm[first:last, dy : dy + height].reshape((last - first) * cells_out, 3 * chans)
            term = jnp.dot(
                left, wconv[lag, dy].reshape(3 * chans, couts), preferred_element_type=f32
            )
            acc = term if acc is None else acc + term
        return acc

    part = pltpu.make_async_remote_copy(
        src_ref=part_out, dst_ref=part_in, send_sem=p_send, recv_sem=p_recv,
        device_id=(lax.rem(k + 1, n_tm), h, w), device_id_type=MESH,
    )
    conv_copies[0].wait()
    lag0 = conv(0, 2, 0)
    acc0[...] = lag0[:cells_out]
    part_out[1] = lag0[cells_out:].astype(bf16)
    conv_copies[1].wait()
    part_out[0] = (acc0[...] + conv(1, 2, 1)).astype(bf16)
    pl.when(k + 1 < n_tm)(part.start)
    acc1[...] = conv(0, 1, 1)
    conv_copies[2].wait()
    lag2 = conv(0, 2, 2) + cbias[...]
    own0 = lag2[:cells_out]
    own1 = lag2[cells_out:] + acc1[...]
    pl.when(k > 0)(part.wait_recv)
    prior0 = jnp.where(k == 0, acc0[...] + acc1[...], part_in[0].astype(f32))
    prior1 = jnp.where(k == 0, acc0[...], part_in[1].astype(f32))
    feat[0] = (own0 + prior0).astype(bf16).reshape(height, breadth, couts)
    feat[1] = (own1 + prior1).astype(bf16).reshape(height, breadth, couts)

    def edge_row(i, carry):
        t, r = i // height, lax.rem(i, height)
        row = feat[t, r].astype(f32)
        fcol_out[0, t, pl.ds(r, 1), :] = row[0:1]
        fcol_out[1, t, pl.ds(r, 1), :] = row[breadth - 1 : breadth]
        return carry

    lax.fori_loop(0, frames * height, edge_row, 0, unroll=4)
    for i, (dy, dx) in enumerate(DIRS[4:]):
        r = 0 if dy < 0 else height - 1
        fcorner_out[i] = fcol_out[0 if dx < 0 else 1, :, r, :]
    fhalos = halo_copies(feat, fcol_out, fcorner_out, frow_in, fcol_in, fcorner_in, f_send, f_recv)
    start_all(fhalos)
    for copy in up_copies:
        copy.wait()
    wait_recv_all(fhalos)

    def feat_row(i, carry):
        t, r = i // height, lax.rem(i, height)
        put_row(
            fpad, t, r + 1, feat[t, r].astype(f32),
            jnp.where(left_ok, fcol_in[0, t, pl.ds(r, 1), :], 0.0),
            jnp.where(right_ok, fcol_in[1, t, pl.ds(r, 1), :], 0.0),
        )
        return carry

    lax.fori_loop(0, frames * height, feat_row, 0, unroll=2)
    for side, row, ok in ((0, 0, up_ok), (1, height + 1, down_ok)):
        for t in range(frames):
            put_row(
                fpad, t, row, jnp.where(ok, frow_in[side, t].astype(f32), 0.0),
                jnp.where(ok & left_ok, fcorner_in[2 * side, t : t + 1, :], 0.0),
                jnp.where(ok & right_ok, fcorner_in[2 * side + 1, t : t + 1, :], 0.0),
            )

    for row_par in (0, 1):
        for col_par in (0, 1):
            acc = None
            for off, kh in (((0, 3), (1, 1)) if row_par == 0 else ((1, 2), (2, 0))):
                left = fpad[:, off : off + height, :, col_par * couts : (col_par + 2) * couts]
                right = wup[kh, 2 * col_par : 2 * col_par + 2].reshape(2 * couts, couts)
                term = jnp.dot(
                    left.reshape(frames * cells_out, 2 * couts), right, preferred_element_type=f32
                )
                acc = term if acc is None else acc + term
            acc = (acc + ubias[...]).reshape(frames, height, breadth, couts)
            for t in range(frames):
                for half in range(couts // 128):
                    lanes = slice(half * 128, half * 128 + 128)
                    spread[half, t, :, row_par, pl.ds(col_par, breadth, stride=2), :] = acc[
                        t, :, :, lanes
                    ]
        for half in range(couts // 128):
            out[:, :, row_par, :, half * 128 : half * 128 + 128] = spread[half, :, :, row_par].astype(
                bf16
            )

    for d in range(1, n_plane):
        plane_copy(d, None).wait_send()
    for d in range(1, n_tm):
        pl.when(k + d < n_tm)(tm_copy(d, k).wait_send)
    wait_send_all(halos)
    pl.when(k + 1 < n_tm)(part.wait_send)
    wait_send_all(fhalos)


def shards(sizes, latent, norm_gain, norm_bias, conv_weight, conv_bias, up_weight, up_bias):
    n_tm, n_ha, n_wa = sizes
    frames, height, breadth, chans = latent.shape
    couts = conv_bias.shape[0]
    f32, bf16 = jnp.float32, jnp.bfloat16
    cells = height * breadth
    vmem = pl.BlockSpec(memory_space=pltpu.VMEM)
    hbm = pl.BlockSpec(memory_space=pl.ANY)
    dma = pltpu.SemaphoreType.DMA
    scratch = [
        pltpu.VMEM(conv_weight.shape, bf16),
        pltpu.VMEM(up_weight.shape, bf16),
        pltpu.VMEM((2, chans), f32),
        pltpu.VMEM((n_ha * n_wa, 2, chans), f32),
        pltpu.VMEM((n_tm, 2, chans), f32),
        pltpu.VMEM((2, frames, height, chans), f32),
        pltpu.VMEM((4, frames, chans), f32),
        pltpu.VMEM((2, frames, breadth, chans), bf16),
        pltpu.VMEM((2, frames, height, chans), f32),
        pltpu.VMEM((4, frames, chans), f32),
        pltpu.VMEM((2, frames, height + 2, chans), f32),
        pltpu.VMEM((frames, height + 2, breadth, 3 * chans), bf16),
        pltpu.VMEM((cells, couts), f32),
        pltpu.VMEM((cells, couts), f32),
        pltpu.VMEM((2, cells, couts), bf16),
        pltpu.VMEM((2, cells, couts), bf16),
        pltpu.VMEM((frames, height, breadth, couts), bf16),
        pltpu.VMEM((2, frames, height, couts), f32),
        pltpu.VMEM((4, frames, couts), f32),
        pltpu.VMEM((2, frames, breadth, couts), bf16),
        pltpu.VMEM((2, frames, height, couts), f32),
        pltpu.VMEM((4, frames, couts), f32),
        pltpu.VMEM((frames, height + 2, breadth, 3 * couts), bf16),
        pltpu.VMEM((couts // 128, frames, height, 2, 2 * breadth, 128), f32),
        dma((3,)), dma((4,)),
        dma((n_ha * n_wa,)), dma((n_ha * n_wa,)),
        dma((n_tm,)), dma((n_tm,)),
        dma((8,)), dma((8,)),
        dma(()), dma(()),
        dma((8,)), dma((8,)),
    ]
    result = pl.pallas_call(
        functools.partial(section_kernel, n_tm, n_ha, n_wa),
        out_shape=jax.ShapeDtypeStruct((frames, height, 2, 2 * breadth, couts), bf16),
        in_specs=[vmem, vmem, vmem, hbm, vmem, hbm, vmem],
        out_specs=vmem,
        scratch_shapes=scratch,
        compiler_params=pltpu.CompilerParams(
            collective_id=0, has_side_effects=True, vmem_limit_bytes=56 * 1024 * 1024
        ),
    )(
        latent, norm_gain[None], norm_bias[None], conv_weight, conv_bias[None], up_weight,
        up_bias[None],
    )
    return result.reshape(frames, 2 * height, 2 * breadth, couts)


def solution(mesh):
    sizes = (mesh.shape["tm"], mesh.shape["ha"], mesh.shape["wa"])
    in_specs = (P("tm", "ha", "wa", None), P(), P(), P(), P(), P(), P())
    out_specs = P("tm", "ha", "wa", None)
    return jax.shard_map(
        functools.partial(shards, sizes), mesh=mesh, in_specs=in_specs, out_specs=out_specs,
        check_vma=False,
    )
```

```python
import functools

import jax
import jax.numpy as jnp
from jax import lax
from jax.experimental import pallas as pl
from jax.experimental.pallas import tpu as pltpu
from jax.sharding import PartitionSpec as P

GROUPS = 32
MESH = pl.DeviceIdType.MESH
DIRS = ((-1, 0), (1, 0), (0, -1), (0, 1), (-1, -1), (-1, 1), (1, -1), (1, 1))


def section_kernel(
    n_tm, n_ha, n_wa,
    lat, gain, nbias, wconv_hbm, cbias, wup_hbm,
    fpad, wup,
    wconv, sums, plane_stats, block_stats,
    col_out, corner_out, row_in, col_in, corner_in, halo_norm, norm,
    acc0, acc1, part_out, part_in,
    feat, fcol_out, fcorner_out, frow_in, fcol_in, fcorner_in,
    wsem, usem, pl_send, pl_recv, tm_send, tm_recv, h_send, h_recv, p_send, p_recv, f_send, f_recv,
):
    f32, bf16 = jnp.float32, jnp.bfloat16
    frames, height, breadth, chans = lat.shape
    couts = cbias.shape[-1]
    k, h, w = lax.axis_index("tm"), lax.axis_index("ha"), lax.axis_index("wa")
    n_plane = n_ha * n_wa
    me = h * n_wa + w

    conv_copies = [
        pltpu.make_async_copy(wconv_hbm.at[lag], wconv.at[lag], wsem.at[lag]) for lag in range(3)
    ]

    def plane_peer(d):
        q = lax.rem(me + d, n_plane)
        return q, (k, q // n_wa, lax.rem(q, n_wa))

    barrier = pltpu.get_barrier_semaphore()
    for d in range(1, n_plane):
        pl.semaphore_signal(barrier, inc=1, device_id=plane_peer(d)[1], device_id_type=MESH)
    for d in range(1, n_tm):
        pl.semaphore_signal(
            barrier, inc=1, device_id=(lax.rem(k + d, n_tm), h, w), device_id_type=MESH
        )
    up_copy = pltpu.make_async_copy(wup_hbm, wup, usem)
    for copy in conv_copies + [up_copy]:
        copy.start()

    def add_row(i, carry):
        total, square = carry
        t, r = i // height, lax.rem(i, height)
        row = lat[t, r].astype(f32)
        col_out[0, t, pl.ds(r, 1), :] = row[0:1]
        col_out[1, t, pl.ds(r, 1), :] = row[breadth - 1 : breadth]
        return total + row, square + row * row

    zero = jnp.zeros((breadth, chans), f32)
    total, square = lax.fori_loop(0, frames * height, add_row, (zero, zero), unroll=4)
    sums[0:1, :] = jnp.sum(total, axis=0, keepdims=True)
    sums[1:2, :] = jnp.sum(square, axis=0, keepdims=True)
    for i, (dy, dx) in enumerate(DIRS[4:]):
        r = 0 if dy < 0 else height - 1
        corner_out[i] = col_out[0 if dx < 0 else 1, :, r, :]
    pl.semaphore_wait(barrier, n_plane - 1 + n_tm - 1)

    def plane_copy(d, slot):
        q, where = plane_peer(d)
        index = me if slot is None else slot
        return pltpu.make_async_remote_copy(
            src_ref=sums, dst_ref=plane_stats.at[index], send_sem=pl_send.at[d],
            recv_sem=pl_recv.at[index], device_id=where, device_id_type=MESH,
        )

    for d in range(1, n_plane):
        plane_copy(d, None).start()
    plane_stats[me] = sums[...]

    def exists(dy, dx):
        ok = None
        for here, step, count in ((h, dy, n_ha), (w, dx, n_wa)):
            if step:
                one = (here + step >= 0) & (here + step < count)
                ok = one if ok is None else ok & one
        return ok

    def halo_copies(tile, cols, corners, rin, cin, kin, send, recv):
        made = []
        for i, (dy, dx) in enumerate(DIRS):
            if dx == 0:
                src, dst = tile.at[:, 0 if dy < 0 else height - 1], rin.at[1 if dy < 0 else 0]
            elif dy == 0:
                src, dst = cols.at[0 if dx < 0 else 1], cin.at[1 if dx < 0 else 0]
            else:
                src, dst = corners.at[i - 4], kin.at[7 - i]
            made.append((dy, dx, pltpu.make_async_remote_copy(
                src_ref=src, dst_ref=dst, send_sem=send.at[i], recv_sem=recv.at[i],
                device_id=(k, h + dy, w + dx), device_id_type=MESH,
            )))
        return made

    def start_all(made):
        for dy, dx, copy in made:
            pl.when(exists(dy, dx))(copy.start)

    def wait_send_all(made):
        for dy, dx, copy in made:
            pl.when(exists(dy, dx))(copy.wait_send)

    def wait_recv_all(made):
        for dy, dx, copy in made:
            pl.when(exists(-dy, -dx))(copy.wait_recv)

    halos = halo_copies(lat, col_out, corner_out, row_in, col_in, corner_in, h_send, h_recv)
    start_all(halos)

    for d in range(1, n_plane):
        plane_copy(d, plane_peer(d)[0]).wait_recv()
    block = plane_stats[0]
    for q in range(1, n_plane):
        block = block + plane_stats[q]
    block_stats[k] = block

    def tm_copy(d, slot):
        return pltpu.make_async_remote_copy(
            src_ref=block_stats.at[k], dst_ref=block_stats.at[slot], send_sem=tm_send.at[d],
            recv_sem=tm_recv.at[slot], device_id=(lax.rem(k + d, n_tm), h, w), device_id_type=MESH,
        )

    for d in range(1, n_tm):
        pl.when(k + d < n_tm)(tm_copy(d, k).start)
    wait_recv_all(halos)
    for d in range(1, n_tm):
        pl.when(k >= d)(tm_copy(d, lax.rem(k + n_tm - d, n_tm)).wait_recv)
    upto = block
    for q in range(n_tm):
        upto = upto + jnp.where(q < k, block_stats[q], 0.0)
    lane = lax.broadcasted_iota(jnp.int32, upto.shape, 1)
    group_width = chans // GROUPS
    step = 1
    while step < group_width:
        ahead = pltpu.roll(upto, chans - step, 1)
        behind = pltpu.roll(upto, step, 1)
        upto = upto + jnp.where((lane & step) == 0, ahead, behind)
        step *= 2
    cells = float(frames * height * breadth * n_plane * group_width)
    stats = upto / ((k + 1).astype(f32) * cells)
    mean = stats[0:1]
    variance = stats[1:2] - mean * mean
    half_scale = 0.5 * (lax.rsqrt(variance + 1e-06) * gain[...])
    half_bias = 0.5 * nbias[...]

    def normed(x):
        half = (x - mean) * half_scale + half_bias
        return half + half * jnp.tanh(half)

    up_ok, down_ok, left_ok, right_ok = exists(-1, 0), exists(1, 0), exists(0, -1), exists(0, 1)
    for side, ok in ((0, left_ok), (1, right_ok)):
        for t in range(frames):
            halo_norm[side, t, 1 : height + 1, :] = jnp.where(ok, normed(col_in[side, t]), 0.0)
    for i, (dy, dx) in enumerate(DIRS[4:]):
        row = 0 if dy < 0 else height + 1
        value = jnp.where(exists(dy, dx), normed(corner_in[i]), 0.0)
        for t in range(frames):
            halo_norm[0 if dx < 0 else 1, t, row : row + 1, :] = value[t : t + 1]

    def put_row(dest, t, r, y, left, right):
        column = lax.broadcasted_iota(jnp.int32, y.shape, 0)
        size = y.shape[1]
        dest[t, r, :, 0:size] = jnp.where(column == 0, left, pltpu.roll(y, 1, 0)).astype(bf16)
        dest[t, r, :, size : 2 * size] = y.astype(bf16)
        dest[t, r, :, 2 * size :] = jnp.where(
            column == breadth - 1, right, pltpu.roll(y, breadth - 1, 0)
        ).astype(bf16)

    def norm_row(i, carry):
        t, r = i // height, lax.rem(i, height)
        put_row(
            norm, t, r + 1, normed(lat[t, r].astype(f32)),
            halo_norm[0, t, pl.ds(r + 1, 1), :], halo_norm[1, t, pl.ds(r + 1, 1), :],
        )
        return carry

    lax.fori_loop(0, frames * height, norm_row, 0, unroll=2)
    for side, row, ok in ((0, 0, up_ok), (1, height + 1, down_ok)):
        for t in range(frames):
            put_row(
                norm, t, row, jnp.where(ok, normed(row_in[side, t].astype(f32)), 0.0),
                halo_norm[0, t, row : row + 1, :], halo_norm[1, t, row : row + 1, :],
            )

    cells_out = height * breadth

    def conv(first, last, lag):
        acc = None
        for dy in range(3):
            left = norm[first:last, dy : dy + height].reshape((last - first) * cells_out, 3 * chans)
            term = jnp.dot(
                left, wconv[lag, dy].reshape(3 * chans, couts), preferred_element_type=f32
            )
            acc = term if acc is None else acc + term
        return acc

    parts = [
        pltpu.make_async_remote_copy(
            src_ref=part_out.at[i], dst_ref=part_in.at[i], send_sem=p_send.at[i],
            recv_sem=p_recv.at[i], device_id=(lax.rem(k + 1, n_tm), h, w), device_id_type=MESH,
        )
        for i in range(2)
    ]
    conv_copies[0].wait()
    lag0 = conv(0, 2, 0)
    part_out[1] = lag0[cells_out:].astype(bf16)
    pl.when(k + 1 < n_tm)(parts[1].start)
    acc0[...] = lag0[:cells_out]
    conv_copies[1].wait()
    lag1 = conv(0, 2, 1)
    part_out[0] = (acc0[...] + lag1[cells_out:]).astype(bf16)
    pl.when(k + 1 < n_tm)(parts[0].start)
    acc1[...] = lag1[:cells_out]
    conv_copies[2].wait()
    lag2 = conv(0, 2, 2) + cbias[...]
    own0 = lag2[:cells_out]
    own1 = lag2[cells_out:] + acc1[...]
    for part in parts:
        pl.when(k > 0)(part.wait_recv)
    prior0 = jnp.where(k == 0, acc0[...] + acc1[...], part_in[0].astype(f32))
    prior1 = jnp.where(k == 0, acc0[...], part_in[1].astype(f32))
    feat[0] = (own0 + prior0).astype(bf16).reshape(height, breadth, couts)
    feat[1] = (own1 + prior1).astype(bf16).reshape(height, breadth, couts)

    def edge_row(i, carry):
        t, r = i // height, lax.rem(i, height)
        row = feat[t, r].astype(f32)
        fcol_out[0, t, pl.ds(r, 1), :] = row[0:1]
        fcol_out[1, t, pl.ds(r, 1), :] = row[breadth - 1 : breadth]
        return carry

    lax.fori_loop(0, frames * height, edge_row, 0, unroll=4)
    for i, (dy, dx) in enumerate(DIRS[4:]):
        r = 0 if dy < 0 else height - 1
        fcorner_out[i] = fcol_out[0 if dx < 0 else 1, :, r, :]
    fhalos = halo_copies(feat, fcol_out, fcorner_out, frow_in, fcol_in, fcorner_in, f_send, f_recv)
    start_all(fhalos)

    def feat_row(i, carry):
        t, r = i // height, lax.rem(i, height)
        put_row(fpad, t, r + 1, feat[t, r].astype(f32), 0.0, 0.0)
        return carry

    lax.fori_loop(0, frames * height, feat_row, 0, unroll=4)
    wait_recv_all(fhalos)
    column = lax.broadcasted_iota(jnp.int32, (breadth, couts), 0)

    def edge_patch(i, carry):
        t, r = i // height, lax.rem(i, height)
        for side, ok, at in ((0, left_ok, 0), (1, right_ok, breadth - 1)):
            lanes = slice(2 * side * couts, (2 * side + 1) * couts)
            mixed = jnp.where(
                (column == at) & ok, fcol_in[side, t, pl.ds(r, 1), :],
                fpad[t, r + 1, :, lanes].astype(f32),
            )
            fpad[t, r + 1, :, lanes] = mixed.astype(bf16)
        return carry

    lax.fori_loop(0, frames * height, edge_patch, 0, unroll=4)
    for side, row, ok in ((0, 0, up_ok), (1, height + 1, down_ok)):
        for t in range(frames):
            put_row(
                fpad, t, row, jnp.where(ok, frow_in[side, t].astype(f32), 0.0),
                jnp.where(ok & left_ok, fcorner_in[2 * side, t : t + 1, :], 0.0),
                jnp.where(ok & right_ok, fcorner_in[2 * side + 1, t : t + 1, :], 0.0),
            )

    up_copy.wait()
    for d in range(1, n_plane):
        plane_copy(d, None).wait_send()
    for d in range(1, n_tm):
        pl.when(k + d < n_tm)(tm_copy(d, k).wait_send)
    wait_send_all(halos)
    for part in parts:
        pl.when(k + 1 < n_tm)(part.wait_send)
    wait_send_all(fhalos)


def upsample_kernel(fpad, wup, ubias, out, spread, ready, sem):
    f32, bf16 = jnp.float32, jnp.bfloat16
    frames, padded, breadth, _ = fpad.shape
    height = padded - 2
    couts = ubias.shape[-1]
    copies = []
    for row_par in (0, 1):
        for col_par in (0, 1):
            acc = None
            for off, kh in (((0, 3), (1, 1)) if row_par == 0 else ((1, 2), (2, 0))):
                left = fpad[:, off : off + height, :, col_par * couts : (col_par + 2) * couts]
                kws = (3, 1) if col_par == 0 else (2, 0)
                right = jnp.concatenate([wup[kh, kw] for kw in kws], axis=0)
                term = jnp.dot(
                    left.reshape(frames * height * breadth, 2 * couts), right,
                    preferred_element_type=f32,
                )
                acc = term if acc is None else acc + term
            acc = (acc + ubias[...]).reshape(frames, height, breadth, couts)
            for half in range(couts // 128):
                spread[half, :, :, row_par, pl.ds(col_par, breadth, stride=2), :] = acc[
                    :, :, :, half * 128 : half * 128 + 128
                ]
        for half in range(couts // 128):
            ready[row_par, :, :, :, half * 128 : half * 128 + 128] = spread[
                half, :, :, row_par
            ].astype(bf16)
        copies.append(pltpu.make_async_copy(ready.at[row_par], out.at[:, :, row_par], sem.at[row_par]))
        copies[-1].start()
    for copy in copies:
        copy.wait()


def shards(sizes, latent, norm_gain, norm_bias, conv_weight, conv_bias, up_weight, up_bias):
    n_tm, n_ha, n_wa = sizes
    frames, height, breadth, chans = latent.shape
    couts = conv_bias.shape[0]
    f32, bf16 = jnp.float32, jnp.bfloat16
    cells = height * breadth
    vmem = pl.BlockSpec(memory_space=pltpu.VMEM)
    hbm = pl.BlockSpec(memory_space=pl.ANY)
    dma = pltpu.SemaphoreType.DMA
    scratch = [
        pltpu.VMEM(conv_weight.shape, bf16),
        pltpu.VMEM((2, chans), f32),
        pltpu.VMEM((n_ha * n_wa, 2, chans), f32),
        pltpu.VMEM((n_tm, 2, chans), f32),
        pltpu.VMEM((2, frames, height, chans), f32),
        pltpu.VMEM((4, frames, chans), f32),
        pltpu.VMEM((2, frames, breadth, chans), bf16),
        pltpu.VMEM((2, frames, height, chans), f32),
        pltpu.VMEM((4, frames, chans), f32),
        pltpu.VMEM((2, frames, height + 2, chans), f32),
        pltpu.VMEM((frames, height + 2, breadth, 3 * chans), bf16),
        pltpu.VMEM((cells, couts), f32),
        pltpu.VMEM((cells, couts), f32),
        pltpu.VMEM((2, cells, couts), bf16),
        pltpu.VMEM((2, cells, couts), bf16),
        pltpu.VMEM((frames, height, breadth, couts), bf16),
        pltpu.VMEM((2, frames, height, couts), f32),
        pltpu.VMEM((4, frames, couts), f32),
        pltpu.VMEM((2, frames, breadth, couts), bf16),
        pltpu.VMEM((2, frames, height, couts), f32),
        pltpu.VMEM((4, frames, couts), f32),
        dma((3,)), dma(()),
        dma((n_ha * n_wa,)), dma((n_ha * n_wa,)),
        dma((n_tm,)), dma((n_tm,)),
        dma((8,)), dma((8,)),
        dma((2,)), dma((2,)),
        dma((8,)), dma((8,)),
    ]
    fpad, wup = pl.pallas_call(
        functools.partial(section_kernel, n_tm, n_ha, n_wa),
        out_shape=[
            jax.ShapeDtypeStruct((frames, height + 2, breadth, 3 * couts), bf16),
            jax.ShapeDtypeStruct(up_weight.shape, bf16),
        ],
        in_specs=[vmem, vmem, vmem, pl.BlockSpec(memory_space=pltpu.HBM), vmem, pl.BlockSpec(memory_space=pltpu.HBM)],
        out_specs=[vmem, vmem],
        scratch_shapes=scratch,
        compiler_params=pltpu.CompilerParams(
            collective_id=0, has_side_effects=True, vmem_limit_bytes=50 * 1024 * 1024
        ),
    )(latent, norm_gain[None], norm_bias[None], conv_weight, conv_bias[None], up_weight)
    result = pl.pallas_call(
        upsample_kernel,
        out_shape=jax.ShapeDtypeStruct((frames, height, 2, 2 * breadth, couts), bf16),
        in_specs=[vmem, vmem, vmem],
        out_specs=pl.BlockSpec(memory_space=pltpu.HBM),
        scratch_shapes=[
            pltpu.VMEM((couts // 128, frames, height, 2, 2 * breadth, 128), f32),
            pltpu.VMEM((2, frames, height, 2 * breadth, couts), bf16),
            dma((2,)),
        ],
        compiler_params=pltpu.CompilerParams(vmem_limit_bytes=20 * 1024 * 1024),
    )(fpad, wup, up_bias[None])
    return result.reshape(frames, 2 * height, 2 * breadth, couts)


def solution(mesh):
    sizes = (mesh.shape["tm"], mesh.shape["ha"], mesh.shape["wa"])
    in_specs = (P("tm", "ha", "wa", None), P(), P(), P(), P(), P(), P())
    out_specs = P("tm", "ha", "wa", None)
    return jax.shard_map(
        functools.partial(shards, sizes), mesh=mesh, in_specs=in_specs, out_specs=out_specs,
        check_vma=False,
    )
```

```python
import functools

import jax
import jax.numpy as jnp
from jax import lax
from jax.experimental import pallas as pl
from jax.experimental.pallas import tpu as pltpu
from jax.sharding import PartitionSpec as P

GROUPS = 32
MESH = pl.DeviceIdType.MESH
DIRS = ((-1, 0), (1, 0), (0, -1), (0, 1), (-1, -1), (-1, 1), (1, -1), (1, 1))


def section_kernel(
    n_tm, n_ha, n_wa,
    lat_hbm, gain_hbm, nbias_hbm, wconv_hbm, cbias_hbm,
    fpad,
    lat, gain, nbias, cbias, wconv, sums, plane_stats, block_stats,
    col_out, corner_out, row_in, col_in, corner_in, halo_norm, norm,
    acc0, acc1, part_out, part_in,
    feat, fcol_out, fcorner_out, frow_in, fcol_in, fcorner_in,
    isem, wsem, pl_send, pl_recv, tm_send, tm_recv, h_send, h_recv, p_send, p_recv, f_send, f_recv,
):
    f32, bf16 = jnp.float32, jnp.bfloat16
    frames, height, breadth, chans = lat.shape
    couts = cbias.shape[-1]
    k, h, w = lax.axis_index("tm"), lax.axis_index("ha"), lax.axis_index("wa")
    n_plane = n_ha * n_wa
    me = h * n_wa + w

    in_copies = [
        pltpu.make_async_copy(source, held, isem.at[i])
        for i, (source, held) in enumerate(
            ((lat_hbm, lat), (gain_hbm, gain), (nbias_hbm, nbias), (cbias_hbm, cbias))
        )
    ]
    for copy in in_copies:
        copy.start()
    conv_copies = [
        pltpu.make_async_copy(wconv_hbm.at[lag], wconv.at[lag], wsem.at[lag]) for lag in range(3)
    ]

    def plane_peer(d):
        q = lax.rem(me + d, n_plane)
        return q, (k, q // n_wa, lax.rem(q, n_wa))

    barrier = pltpu.get_barrier_semaphore()
    for d in range(1, n_plane):
        pl.semaphore_signal(barrier, inc=1, device_id=plane_peer(d)[1], device_id_type=MESH)
    for d in range(1, n_tm):
        pl.semaphore_signal(
            barrier, inc=1, device_id=(lax.rem(k + d, n_tm), h, w), device_id_type=MESH
        )
    for copy in conv_copies:
        copy.start()

    for copy in in_copies:
        copy.wait()

    def add_row(i, carry):
        total, square = carry
        t, r = i // height, lax.rem(i, height)
        row = lat[t, r].astype(f32)
        col_out[0, t, pl.ds(r, 1), :] = row[0:1]
        col_out[1, t, pl.ds(r, 1), :] = row[breadth - 1 : breadth]
        return total + row, square + row * row

    zero = jnp.zeros((breadth, chans), f32)
    total, square = lax.fori_loop(0, frames * height, add_row, (zero, zero), unroll=4)
    sums[0:1, :] = jnp.sum(total, axis=0, keepdims=True)
    sums[1:2, :] = jnp.sum(square, axis=0, keepdims=True)
    for i, (dy, dx) in enumerate(DIRS[4:]):
        r = 0 if dy < 0 else height - 1
        corner_out[i] = col_out[0 if dx < 0 else 1, :, r, :]
    pl.semaphore_wait(barrier, n_plane - 1 + n_tm - 1)

    def plane_copy(d, slot):
        q, where = plane_peer(d)
        index = me if slot is None else slot
        return pltpu.make_async_remote_copy(
            src_ref=sums, dst_ref=plane_stats.at[index], send_sem=pl_send.at[d],
            recv_sem=pl_recv.at[index], device_id=where, device_id_type=MESH,
        )

    for d in range(1, n_plane):
        plane_copy(d, None).start()
    plane_stats[me] = sums[...]

    def exists(dy, dx):
        ok = None
        for here, step, count in ((h, dy, n_ha), (w, dx, n_wa)):
            if step:
                one = (here + step >= 0) & (here + step < count)
                ok = one if ok is None else ok & one
        return ok

    def halo_copies(tile, cols, corners, rin, cin, kin, send, recv):
        made = []
        for i, (dy, dx) in enumerate(DIRS):
            if dx == 0:
                src, dst = tile.at[:, 0 if dy < 0 else height - 1], rin.at[1 if dy < 0 else 0]
            elif dy == 0:
                src, dst = cols.at[0 if dx < 0 else 1], cin.at[1 if dx < 0 else 0]
            else:
                src, dst = corners.at[i - 4], kin.at[7 - i]
            made.append((dy, dx, pltpu.make_async_remote_copy(
                src_ref=src, dst_ref=dst, send_sem=send.at[i], recv_sem=recv.at[i],
                device_id=(k, h + dy, w + dx), device_id_type=MESH,
            )))
        return made

    def start_all(made):
        for dy, dx, copy in made:
            pl.when(exists(dy, dx))(copy.start)

    def wait_send_all(made):
        for dy, dx, copy in made:
            pl.when(exists(dy, dx))(copy.wait_send)

    def wait_recv_all(made):
        for dy, dx, copy in made:
            pl.when(exists(-dy, -dx))(copy.wait_recv)

    halos = halo_copies(lat, col_out, corner_out, row_in, col_in, corner_in, h_send, h_recv)
    start_all(halos)

    for d in range(1, n_plane):
        plane_copy(d, plane_peer(d)[0]).wait_recv()
    block = plane_stats[0]
    for q in range(1, n_plane):
        block = block + plane_stats[q]
    block_stats[k] = block

    def tm_copy(d, slot):
        return pltpu.make_async_remote_copy(
            src_ref=block_stats.at[k], dst_ref=block_stats.at[slot], send_sem=tm_send.at[d],
            recv_sem=tm_recv.at[slot], device_id=(lax.rem(k + d, n_tm), h, w), device_id_type=MESH,
        )

    for d in range(1, n_tm):
        pl.when(k + d < n_tm)(tm_copy(d, k).start)
    wait_recv_all(halos)
    for d in range(1, n_tm):
        pl.when(k >= d)(tm_copy(d, lax.rem(k + n_tm - d, n_tm)).wait_recv)
    upto = block
    for q in range(n_tm):
        upto = upto + jnp.where(q < k, block_stats[q], 0.0)
    lane = lax.broadcasted_iota(jnp.int32, upto.shape, 1)
    group_width = chans // GROUPS
    step = 1
    while step < group_width:
        ahead = pltpu.roll(upto, chans - step, 1)
        behind = pltpu.roll(upto, step, 1)
        upto = upto + jnp.where((lane & step) == 0, ahead, behind)
        step *= 2
    cells = float(frames * height * breadth * n_plane * group_width)
    stats = upto / ((k + 1).astype(f32) * cells)
    mean = stats[0:1]
    variance = stats[1:2] - mean * mean
    half_scale = 0.5 * (lax.rsqrt(variance + 1e-06) * gain[...])
    half_bias = 0.5 * nbias[...]

    def normed(x):
        half = (x - mean) * half_scale + half_bias
        return half + half * jnp.tanh(half)

    up_ok, down_ok, left_ok, right_ok = exists(-1, 0), exists(1, 0), exists(0, -1), exists(0, 1)
    for side, ok in ((0, left_ok), (1, right_ok)):
        for t in range(frames):
            halo_norm[side, t, 1 : height + 1, :] = jnp.where(ok, normed(col_in[side, t]), 0.0)
    for i, (dy, dx) in enumerate(DIRS[4:]):
        row = 0 if dy < 0 else height + 1
        value = jnp.where(exists(dy, dx), normed(corner_in[i]), 0.0)
        for t in range(frames):
            halo_norm[0 if dx < 0 else 1, t, row : row + 1, :] = value[t : t + 1]

    def put_row(dest, t, r, y, left, right):
        column = lax.broadcasted_iota(jnp.int32, y.shape, 0)
        size = y.shape[1]
        dest[t, r, :, 0:size] = jnp.where(column == 0, left, pltpu.roll(y, 1, 0)).astype(bf16)
        dest[t, r, :, size : 2 * size] = y.astype(bf16)
        dest[t, r, :, 2 * size :] = jnp.where(
            column == breadth - 1, right, pltpu.roll(y, breadth - 1, 0)
        ).astype(bf16)

    def norm_row(i, carry):
        t, r = i // height, lax.rem(i, height)
        put_row(
            norm, t, r + 1, normed(lat[t, r].astype(f32)),
            halo_norm[0, t, pl.ds(r + 1, 1), :], halo_norm[1, t, pl.ds(r + 1, 1), :],
        )
        return carry

    lax.fori_loop(0, frames * height, norm_row, 0, unroll=2)
    for side, row, ok in ((0, 0, up_ok), (1, height + 1, down_ok)):
        for t in range(frames):
            put_row(
                norm, t, row, jnp.where(ok, normed(row_in[side, t].astype(f32)), 0.0),
                halo_norm[0, t, row : row + 1, :], halo_norm[1, t, row : row + 1, :],
            )

    cells_out = height * breadth

    def conv(first, last, lag):
        acc = None
        for dy in range(3):
            left = norm[first:last, dy : dy + height].reshape((last - first) * cells_out, 3 * chans)
            term = jnp.dot(
                left, wconv[lag, dy].reshape(3 * chans, couts), preferred_element_type=f32
            )
            acc = term if acc is None else acc + term
        return acc

    parts = [
        pltpu.make_async_remote_copy(
            src_ref=part_out.at[i], dst_ref=part_in.at[i], send_sem=p_send.at[i],
            recv_sem=p_recv.at[i], device_id=(lax.rem(k + 1, n_tm), h, w), device_id_type=MESH,
        )
        for i in range(2)
    ]
    conv_copies[0].wait()
    lag0 = conv(0, 2, 0)
    part_out[1] = lag0[cells_out:].astype(bf16)
    pl.when(k + 1 < n_tm)(parts[1].start)
    acc0[...] = lag0[:cells_out]
    conv_copies[1].wait()
    lag1 = conv(0, 2, 1)
    part_out[0] = (acc0[...] + lag1[cells_out:]).astype(bf16)
    pl.when(k + 1 < n_tm)(parts[0].start)
    acc1[...] = lag1[:cells_out]
    conv_copies[2].wait()
    lag2 = conv(0, 2, 2) + cbias[...]
    own0 = lag2[:cells_out]
    own1 = lag2[cells_out:] + acc1[...]
    for part in parts:
        pl.when(k > 0)(part.wait_recv)
    prior0 = jnp.where(k == 0, acc0[...] + acc1[...], part_in[0].astype(f32))
    prior1 = jnp.where(k == 0, acc0[...], part_in[1].astype(f32))
    feat[0] = (own0 + prior0).astype(bf16).reshape(height, breadth, couts)
    feat[1] = (own1 + prior1).astype(bf16).reshape(height, breadth, couts)

    def edge_row(i, carry):
        t, r = i // height, lax.rem(i, height)
        row = feat[t, r].astype(f32)
        fcol_out[0, t, pl.ds(r, 1), :] = row[0:1]
        fcol_out[1, t, pl.ds(r, 1), :] = row[breadth - 1 : breadth]
        return carry

    lax.fori_loop(0, frames * height, edge_row, 0, unroll=4)
    for i, (dy, dx) in enumerate(DIRS[4:]):
        r = 0 if dy < 0 else height - 1
        fcorner_out[i] = fcol_out[0 if dx < 0 else 1, :, r, :]
    fhalos = halo_copies(feat, fcol_out, fcorner_out, frow_in, fcol_in, fcorner_in, f_send, f_recv)
    start_all(fhalos)

    def feat_row(i, carry):
        t, r = i // height, lax.rem(i, height)
        put_row(fpad, t, r + 1, feat[t, r].astype(f32), 0.0, 0.0)
        return carry

    lax.fori_loop(0, frames * height, feat_row, 0, unroll=4)
    wait_recv_all(fhalos)
    column = lax.broadcasted_iota(jnp.int32, (breadth, couts), 0)

    def edge_patch(i, carry):
        t, r = i // height, lax.rem(i, height)
        for side, ok, at in ((0, left_ok, 0), (1, right_ok, breadth - 1)):
            lanes = slice(2 * side * couts, (2 * side + 1) * couts)
            mixed = jnp.where(
                (column == at) & ok, fcol_in[side, t, pl.ds(r, 1), :],
                fpad[t, r + 1, :, lanes].astype(f32),
            )
            fpad[t, r + 1, :, lanes] = mixed.astype(bf16)
        return carry

    lax.fori_loop(0, frames * height, edge_patch, 0, unroll=4)
    for side, row, ok in ((0, 0, up_ok), (1, height + 1, down_ok)):
        for t in range(frames):
            put_row(
                fpad, t, row, jnp.where(ok, frow_in[side, t].astype(f32), 0.0),
                jnp.where(ok & left_ok, fcorner_in[2 * side, t : t + 1, :], 0.0),
                jnp.where(ok & right_ok, fcorner_in[2 * side + 1, t : t + 1, :], 0.0),
            )

    for d in range(1, n_plane):
        plane_copy(d, None).wait_send()
    for d in range(1, n_tm):
        pl.when(k + d < n_tm)(tm_copy(d, k).wait_send)
    wait_send_all(halos)
    for part in parts:
        pl.when(k + 1 < n_tm)(part.wait_send)
    wait_send_all(fhalos)


def upsample_kernel(fpad, wup, ubias, out, spread, ready, sem):
    f32, bf16 = jnp.float32, jnp.bfloat16
    frames, padded, breadth, _ = fpad.shape
    height = padded - 2
    couts = ubias.shape[-1]
    copies = []
    for row_par in (0, 1):
        for col_par in (0, 1):
            acc = None
            for off, kh in (((0, 3), (1, 1)) if row_par == 0 else ((1, 2), (2, 0))):
                left = fpad[:, off : off + height, :, col_par * couts : (col_par + 2) * couts]
                kws = (3, 1) if col_par == 0 else (2, 0)
                right = jnp.concatenate([wup[kh, kw] for kw in kws], axis=0)
                term = jnp.dot(
                    left.reshape(frames * height * breadth, 2 * couts), right,
                    preferred_element_type=f32,
                )
                acc = term if acc is None else acc + term
            acc = (acc + ubias[...]).reshape(frames, height, breadth, couts)
            for half in range(couts // 128):
                spread[half, :, :, row_par, pl.ds(col_par, breadth, stride=2), :] = acc[
                    :, :, :, half * 128 : half * 128 + 128
                ]
        for half in range(couts // 128):
            ready[row_par, :, :, :, half * 128 : half * 128 + 128] = spread[
                half, :, :, row_par
            ].astype(bf16)
        copies.append(pltpu.make_async_copy(ready.at[row_par], out.at[:, :, row_par], sem.at[row_par]))
        copies[-1].start()
    for copy in copies:
        copy.wait()


def shards(sizes, latent, norm_gain, norm_bias, conv_weight, conv_bias, up_weight, up_bias):
    n_tm, n_ha, n_wa = sizes
    frames, height, breadth, chans = latent.shape
    couts = conv_bias.shape[0]
    f32, bf16 = jnp.float32, jnp.bfloat16
    cells = height * breadth
    vmem = pl.BlockSpec(memory_space=pltpu.VMEM)
    hbm = pl.BlockSpec(memory_space=pl.ANY)
    dma = pltpu.SemaphoreType.DMA
    scratch = [
        pltpu.VMEM(latent.shape, bf16),
        pltpu.VMEM((1, chans), f32),
        pltpu.VMEM((1, chans), f32),
        pltpu.VMEM((1, couts), f32),
        pltpu.VMEM(conv_weight.shape, bf16),
        pltpu.VMEM((2, chans), f32),
        pltpu.VMEM((n_ha * n_wa, 2, chans), f32),
        pltpu.VMEM((n_tm, 2, chans), f32),
        pltpu.VMEM((2, frames, height, chans), f32),
        pltpu.VMEM((4, frames, chans), f32),
        pltpu.VMEM((2, frames, breadth, chans), bf16),
        pltpu.VMEM((2, frames, height, chans), f32),
        pltpu.VMEM((4, frames, chans), f32),
        pltpu.VMEM((2, frames, height + 2, chans), f32),
        pltpu.VMEM((frames, height + 2, breadth, 3 * chans), bf16),
        pltpu.VMEM((cells, couts), f32),
        pltpu.VMEM((cells, couts), f32),
        pltpu.VMEM((2, cells, couts), bf16),
        pltpu.VMEM((2, cells, couts), bf16),
        pltpu.VMEM((frames, height, breadth, couts), bf16),
        pltpu.VMEM((2, frames, height, couts), f32),
        pltpu.VMEM((4, frames, couts), f32),
        pltpu.VMEM((2, frames, breadth, couts), bf16),
        pltpu.VMEM((2, frames, height, couts), f32),
        pltpu.VMEM((4, frames, couts), f32),
        dma((4,)), dma((3,)),
        dma((n_ha * n_wa,)), dma((n_ha * n_wa,)),
        dma((n_tm,)), dma((n_tm,)),
        dma((8,)), dma((8,)),
        dma((2,)), dma((2,)),
        dma((8,)), dma((8,)),
    ]
    fpad = pl.pallas_call(
        functools.partial(section_kernel, n_tm, n_ha, n_wa),
        out_shape=jax.ShapeDtypeStruct((frames, height + 2, breadth, 3 * couts), bf16),
        in_specs=[pl.BlockSpec(memory_space=pltpu.HBM)] * 5,
        out_specs=vmem,
        scratch_shapes=scratch,
        compiler_params=pltpu.CompilerParams(
            collective_id=0, has_side_effects=True, vmem_limit_bytes=57 * 1024 * 1024
        ),
    )(latent, norm_gain[None], norm_bias[None], conv_weight, conv_bias[None])
    result = pl.pallas_call(
        upsample_kernel,
        out_shape=jax.ShapeDtypeStruct((frames, height, 2, 2 * breadth, couts), bf16),
        in_specs=[vmem, vmem, vmem],
        out_specs=pl.BlockSpec(memory_space=pltpu.HBM),
        scratch_shapes=[
            pltpu.VMEM((couts // 128, frames, height, 2, 2 * breadth, 128), f32),
            pltpu.VMEM((2, frames, height, 2 * breadth, couts), bf16),
            dma((2,)),
        ],
        compiler_params=pltpu.CompilerParams(vmem_limit_bytes=20 * 1024 * 1024),
    )(fpad, up_weight, up_bias[None])
    return result.reshape(frames, 2 * height, 2 * breadth, couts)


def solution(mesh):
    sizes = (mesh.shape["tm"], mesh.shape["ha"], mesh.shape["wa"])
    in_specs = (P("tm", "ha", "wa", None), P(), P(), P(), P(), P(), P())
    out_specs = P("tm", "ha", "wa", None)
    return jax.shard_map(
        functools.partial(shards, sizes), mesh=mesh, in_specs=in_specs, out_specs=out_specs,
        check_vma=False,
    )
```
